512 devices in a mesh: aperture: 64 (over z, y_lo, x), tile: 8 (over y_hi, core).
Axes of the slice: x: 4, y: 8 (y_hi: 4, y_lo: 2; y = y_hi * 2 + y_lo), z: 8, core: 2. Of those that a mesh axis runs over, the one named last changes fastest.
Arguments:
- echoes: bfloat16 [2, 1024, 32768], P(None, 'aperture', 'tile'), may hold values from -6 to 6
- taps: bfloat16 [2, 4096], replicated, may hold values from -0.0625 to 0.0625
- steering: bfloat16 [2, 1024, 16], P(None, 'aperture'), may hold values from -1 to 1
- coefficients: float32 [2, 2, 2, 1024, 4], P(None, None, None, 'aperture'), may hold values from -2.5 to 2.5
- offsets: int32 [2, 2, 1024], P(None, None, 'aperture'), may hold values from 0 to 12
Outputs:
- image: float32 [2, 1024, 32768], P(None, 'aperture', 'tile')
The draws below stay inside these ranges and needn't reach their ends.
Inputs may be any that keep to these rules, and one draw needn't show every extreme that they name: offsets + 3 is below 16.
All inputs are finite; a program needn't handle non-finite values.
Results may differ from the reference program's by a relative error of at most 0.0003.
Values may be sent and summed in bfloat16 or wider, within the bound.
A program may use at most 192 MiB of HBM per device.

```python
import jax
import jax.numpy as jnp
from jax import lax

P_DEV = 16
TAPS = 4096
NB = 16
BAND = 4
MERGES = 2
PULSES = 1024
RANGE = 32768
BEAMS = 1024
N_APERTURE = 64


def place_ends(array, own_key, smallest, top_value):
    longest = array.shape.index(max(array.shape))
    spots = []
    for shift in (0, 1):
        where = [jax.random.randint(jax.random.fold_in(own_key, axis), (), 0, length) for axis, length in enumerate(array.shape)]
        where[longest] = (where[longest] + shift) % array.shape[longest]
        spots.append(tuple(where))
    return array.at[spots[0]].set(smallest).at[spots[1]].set(top_value)


def block_levels(stream_key, shape, split, low, largest):
    level, own = 1.0, jax.random.fold_in(stream_key, 6)
    for axis_at, blocks in split:
        steps = jnp.exp(jax.random.uniform(jax.random.fold_in(own, axis_at), (blocks,), jnp.float32, low / len(split), largest / len(split)))
        level = level * jnp.repeat(steps, shape[axis_at] // blocks).reshape([-1 if axis == axis_at else 1 for axis in range(len(shape))])
    return level


def noise(stream_key, extent, width, bound, split=(), held_as=jnp.bfloat16):
    factor_of = block_levels(stream_key, extent, split, -0.22, 0.18) if split else 1.0
    entries = jax.random.normal(stream_key, extent, jnp.float32) * width * factor_of
    return jnp.minimum(jnp.maximum(entries, -bound), bound).astype(held_as)


def setup_inputs(seed: int = 0) -> dict:
    key_of = jax.random.split(jax.random.key(seed), 6)
    echoes = noise(key_of[0], (2, PULSES, RANGE), 1.0, 6.0, ((1, 64), (2, 8)))
    taps = noise(key_of[1], (2, TAPS), (2 * TAPS) ** -0.5, 0.0625)
    steering = noise(key_of[2], (2, PULSES, NB), (2 * P_DEV) ** -0.5, 1.0, ((1, 64),))
    coefficients = noise(key_of[3], (MERGES, 2, 2, BEAMS, BAND), 0.35, 2.5, ((3, 64),), jnp.float32)
    offsets = place_ends(jax.random.randint(key_of[4], (MERGES, 2, BEAMS), 0, NB - BAND + 1), jax.random.fold_in(key_of[4], 1), 0, NB - BAND).astype(jnp.int32)
    return {"echoes": echoes, "taps": taps, "steering": steering, "coefficients": coefficients, "offsets": offsets}


def band_matrix(coef, offs, rows):
    starts = offs[:, None] + jnp.arange(coef.shape[-1], dtype=jnp.int32)[None, :]
    onehot = (starts[:, :, None] == jnp.arange(rows, dtype=jnp.int32)[None, None, :]).astype(jnp.float32)
    return jnp.einsum("cjt,jti->cji", coef.astype(jnp.float32), onehot, precision=lax.Precision.HIGHEST)


def reference(echoes, taps, steering, coefficients, offsets):
    hp = lax.Precision.HIGHEST
    x = echoes.astype(jnp.float32).reshape(2, N_APERTURE, P_DEV, RANGE)
    st = steering.astype(jnp.float32).reshape(2, N_APERTURE, P_DEV, NB)
    real_part = jnp.einsum("dpb,dpr->dbr", st[0], x[0], precision=hp) - jnp.einsum("dpb,dpr->dbr", st[1], x[1], precision=hp)
    imag_part = jnp.einsum("dpb,dpr->dbr", st[0], x[1], precision=hp) + jnp.einsum("dpb,dpr->dbr", st[1], x[0], precision=hp)
    length = 2 * RANGE
    signal = lax.complex(real_part, imag_part)
    tap_f = taps.astype(jnp.float32)[:, ::-1]
    kernel = lax.complex(tap_f[0], tap_f[1])
    full = jnp.fft.ifft(jnp.fft.fft(signal, length, axis=-1) * jnp.fft.fft(kernel, length)[None, None, :], axis=-1)
    full = full[:, :, TAPS - 1:TAPS - 1 + RANGE]
    image = jnp.stack([jnp.real(full), jnp.imag(full)]).astype(jnp.float32)
    index = jnp.arange(N_APERTURE, dtype=jnp.int32)
    for section in range(MERGES):
        partner = jnp.take(image, jnp.bitwise_xor(index, 1 << section), axis=1)
        result = jnp.zeros_like(image)
        for source, data in ((0, image), (1, partner)):
            coef = coefficients[section, source].reshape(2, N_APERTURE, NB, BAND)
            offs = offsets[section, source].reshape(N_APERTURE, NB)
            mats = jax.vmap(lambda c, o: band_matrix(c, o, NB), in_axes=(1, 0), out_axes=1)(coef, offs)
            new_re = jnp.einsum("dji,dir->djr", mats[0], data[0], precision=hp) - jnp.einsum("dji,dir->djr", mats[1], data[1], precision=hp)
            new_im = jnp.einsum("dji,dir->djr", mats[0], data[1], precision=hp) + jnp.einsum("dji,dir->djr", mats[1], data[0], precision=hp)
            result = result + jnp.stack([new_re, new_im])
        image = result
    return image.reshape(2, BEAMS, RANGE)
```

```python
import jax
import jax.numpy as jnp
from jax import lax
from jax.experimental import pallas as pl
from jax.experimental.pallas import tpu as pltpu
from jax.sharding import PartitionSpec as P

BLOCK = 256
STEP = 1024
NB = 16
BAND = 4
MESH = pl.DeviceIdType.MESH
EXACT = lax.Precision.HIGHEST
NT = (((1,), (1,)), ((), ()))


def kernel(n_tile, x_ref, taps_ref, steer_ref, coef_ref, offs_ref, out_ref,
           gathered, toep, rows, acc, mats, views,
           x_send, x_recv, h_send, h_recv, p_send, p_recv):
    width = x_ref.shape[2]
    span = taps_ref.shape[1]
    chunks = width // STEP
    per = STEP // BLOCK
    rows_step = per * 64
    lags = span // STEP
    d = lax.axis_index("aperture")
    t = lax.axis_index("tile")
    x = lax.rem(d, 4)
    base = d - x
    mate = (d, base + x + 1 - 2 * lax.rem(x, 2), base + lax.rem(x + 2, 4), base + 3 - x)
    before = lax.rem(t + n_tile - 1, n_tile)
    after = lax.rem(t + 1, n_tile)

    barrier = pltpu.get_barrier_semaphore()
    for r in (1, 2, 3):
        pl.semaphore_signal(barrier, inc=1, device_id=(mate[r], t), device_id_type=MESH)
    for other in (before, after):
        pl.semaphore_signal(barrier, inc=1, device_id=(d, other), device_id_type=MESH)

    lane = lax.broadcasted_iota(jnp.int32, (NB, 128), 1)
    within = lax.rem(lane, 16).astype(jnp.float32)
    first = lax.rem(lane, 32) < 16
    eye = lax.broadcasted_iota(jnp.int32, (NB, NB), 0) == lax.broadcasted_iota(
        jnp.int32, (NB, NB), 1
    )

    def embedded(s, k):
        row = offs_ref[s][k : k + 1, :].astype(jnp.float32)
        start = jnp.sum(jnp.where(eye, row, 0.0), axis=1, keepdims=True)
        real = coef_ref[s, k, 0]
        imag = coef_ref[s, k, 1]
        top = jnp.zeros((NB, 128), jnp.float32)
        low = jnp.zeros((NB, 128), jnp.float32)
        for b in range(BAND):
            hit = within == start + float(b)
            re = real[:, b : b + 1]
            im = imag[:, b : b + 1]
            top += jnp.where(hit, jnp.where(first, re, -im), 0.0)
            low += jnp.where(hit, jnp.where(first, im, re), 0.0)
        return jnp.concatenate([top, low], axis=0)

    group = lax.broadcasted_iota(jnp.int32, (32, 128), 1) // 32
    mats[0] = jnp.where(group == 0, embedded(0, 0), jnp.where(group == 1, embedded(0, 1), 0.0))
    brow = lax.broadcasted_iota(jnp.int32, (NB, 128), 0)
    place0 = jnp.where((lax.rem(lane, 32) == brow) & (lane < 64), 1.0, 0.0).astype(jnp.bfloat16)
    place1 = jnp.where((lax.rem(lane, 32) == brow + 16) & (lane < 64), 1.0, 0.0).astype(
        jnp.bfloat16
    )
    s_re, s_im = steer_ref[0], steer_ref[1]

    def put(value, where):
        return jnp.dot(value, where, preferred_element_type=jnp.float32)

    views[0] = jnp.concatenate(
        [put(s_re, place0) + put(s_im, place1), put(s_re, place1) - put(s_im, place0)], axis=0
    )

    pl.semaphore_wait(barrier, 5)

    def remote(src, dst, send, recv, where):
        return pltpu.make_async_remote_copy(
            src_ref=src, dst_ref=dst, send_sem=send, recv_sem=recv,
            device_id=where, device_id_type=MESH,
        )

    small = [
        remote(views.at[0], views.at[r], p_send.at[r], p_recv.at[r], (mate[r], t))
        for r in (1, 2, 3)
    ]
    small.append(remote(mats.at[0], mats.at[1], p_send.at[0], p_recv.at[0], (mate[2], t)))

    def own(c, r):
        at = pl.ds(c * STEP, STEP)
        return remote(
            x_ref.at[:, :, at], gathered.at[r, :, :, at], x_send.at[r, c], x_recv.at[r, c],
            (mate[r], t),
        )

    def onward(c):
        at = pl.ds(c * STEP, STEP)
        came, goes = (1, 3) if c % 2 == 0 else (3, 1)
        return remote(
            gathered.at[came, :, :, at], gathered.at[2, :, :, at], x_send.at[2, c],
            x_recv.at[2, c], (mate[goes], t),
        )

    def halo(q):
        return remote(
            rows.at[pl.ds(q * rows_step, rows_step), :],
            rows.at[pl.ds((q + chunks) * rows_step, rows_step), :],
            h_send.at[q], h_recv.at[q], (d, before),
        )

    for copy in small:
        copy.start()
    for c in range(2):
        for r in (1, 3):
            own(c, r).start()

    def build(part, lo, hi):
        line = taps_ref[part : part + 1, :].astype(jnp.float32)
        padded = jnp.concatenate(
            [jnp.zeros((1, 128), jnp.float32), line, jnp.zeros((1, 256), jnp.float32)], axis=1
        )
        wide = jnp.broadcast_to(padded, (16, span + 384))
        for s in range(lo, hi):
            turned = pltpu.roll(wide, s * 16, 1, stride=1, stride_axis=0).astype(jnp.bfloat16)
            toep[part, pl.ds(s * 16, 16), :] = turned[:, 128:]
            toep[part, pl.ds(128 + s * 16, 16), :] = turned[:, : span + 256]

    def stage(q):
        for g in range(chunks):
            lag = q - g
            if lag < 0 or lag > lags:
                continue
            lo, hi = (0, 0) if lag == 0 else ((lag - 1) * per + 1, lag * per)
            left = jnp.concatenate(
                [rows[pl.ds((g * per + k) * 64, rows_step), :] for k in range(lo, hi + 1)], axis=1
            )
            for part in range(2):
                term = lax.dot_general(
                    left, toep[part, :, pl.ds(lo * BLOCK, (hi + 1 - lo) * BLOCK)], NT,
                    preferred_element_type=jnp.float32,
                )
                if lag == 0:
                    acc[part, pl.ds(g * rows_step, rows_step), :] = term
                else:
                    acc[part, pl.ds(g * rows_step, rows_step), :] += term

    def finish(g):
        for i in range(per):
            at = (g * per + i) * 64
            by_re = acc[0, pl.ds(at, 32), :] + acc[0, pl.ds(at + 32, 32), :]
            by_im = acc[1, pl.ds(at, 32), :] + acc[1, pl.ds(at + 32, 32), :]
            to = pl.ds((g * per + i) * BLOCK, BLOCK)
            out_ref[0, :, to] = by_re[:NB] - by_im[NB:]
            out_ref[1, :, to] = by_re[NB:] + by_im[:NB]

    build(0, 0, 4)

    last0 = embedded(1, 0)[:, :32]
    last1 = embedded(1, 1)[:, :32]
    for copy in small:
        copy.wait_recv()
    pair = (
        jnp.dot(last0, mats[0], precision=EXACT, preferred_element_type=jnp.float32),
        jnp.dot(last1, mats[1], precision=EXACT, preferred_element_type=jnp.float32),
    )
    view = views[...].reshape(128, 128)
    weights = jnp.zeros((32, 128), jnp.float32)
    for r in range(4):
        chosen = jnp.where(group == r % 2, pair[r // 2], 0.0)
        whole = lax.dot_general(
            chosen, view, NT, precision=EXACT, preferred_element_type=jnp.float32
        )
        weights = jnp.where(group == r, whole, weights)
    w_high = weights.astype(jnp.bfloat16)
    w_low = (weights - w_high.astype(jnp.float32)).astype(jnp.bfloat16)
    w_both = jnp.concatenate([w_high, w_low], axis=0)

    def pass_on(c):
        for r in (1, 3):
            own(c, r).wait_recv()
        onward(c).start()
        if c + 2 < chunks:
            for r in (1, 3):
                own(c + 2, r).start()

    def combine(c):
        onward(c).wait_recv()
        at = pl.ds(c * STEP, STEP)
        data = jnp.concatenate(
            [x_ref[:, :, at].reshape(32, STEP)]
            + [gathered[r, :, :, at].reshape(32, STEP) for r in (1, 2, 3)],
            axis=0,
        )
        both = jnp.dot(w_both, data, preferred_element_type=jnp.float32)
        value = both[:32] + both[32:]
        high = value.astype(jnp.bfloat16)
        low = (value - high.astype(jnp.float32)).astype(jnp.bfloat16)
        for i in range(per):
            lanes = slice(i * BLOCK, (i + 1) * BLOCK)
            rows[pl.ds((c * per + i) * 64, 32), :] = high[:, lanes]
            rows[pl.ds((c * per + i) * 64 + 32, 32), :] = low[:, lanes]

    pass_on(0)
    build(0, 4, 8)
    pass_on(1)
    build(1, 0, 8)
    for c in range(chunks):
        combine(c)

        @pl.when(t > 0)
        def _():
            halo(c).start()

        if c + 2 < chunks:
            pass_on(c + 2)
        stage(c)

    for q in range(chunks):
        @pl.when(t < n_tile - 1)
        def _():
            halo(q).wait_recv()

        @pl.when(t == n_tile - 1)
        def _():
            rows[pl.ds((q + chunks) * rows_step, rows_step), :] = jnp.zeros(
                (rows_step, BLOCK), jnp.bfloat16
            )

        stage(q + chunks)
        finish(q)

    for copy in small:
        copy.wait_send()
    for c in range(chunks):
        for r in (1, 3):
            own(c, r).wait_send()
        onward(c).wait_send()

        @pl.when(t > 0)
        def _():
            halo(c).wait_send()


def on_device(echoes, taps, steering, coefficients, offsets):
    width, span = echoes.shape[2], taps.shape[1]
    chunks = width // STEP
    blocks = (width + span) // BLOCK
    n_tile = lax.axis_size("tile")
    vmem = pl.BlockSpec(memory_space=pltpu.VMEM)
    dma = pltpu.SemaphoreType.DMA

    def body(*refs):
        kernel(n_tile, *refs)

    return pl.pallas_call(
        body,
        out_shape=jax.ShapeDtypeStruct((2, NB, width), jnp.float32),
        in_specs=[vmem] * 5,
        out_specs=vmem,
        scratch_shapes=[
            pltpu.VMEM((4, 2, NB, width), jnp.bfloat16),
            pltpu.VMEM((2, BLOCK, span + BLOCK), jnp.bfloat16),
            pltpu.VMEM((blocks * 64, BLOCK), jnp.bfloat16),
            pltpu.VMEM((2, width // BLOCK * 64, BLOCK), jnp.float32),
            pltpu.VMEM((2, 32, 128), jnp.float32),
            pltpu.VMEM((4, 32, 128), jnp.float32),
            dma((4, chunks)),
            dma((4, chunks)),
            dma((chunks,)),
            dma((chunks,)),
            dma((4,)),
            dma((4,)),
        ],
        compiler_params=pltpu.CompilerParams(
            collective_id=0, has_side_effects=True, vmem_limit_bytes=48 * 1024 * 1024
        ),
        cost_estimate=pl.CostEstimate(
            flops=2 * 1024 * 256 * 256 * 34 * 2, bytes_accessed=1 << 20, transcendentals=0
        ),
        name="backproject",
    )(echoes, taps, steering, coefficients, offsets)


def solution(mesh):
    in_specs = (
        P(None, "aperture", "tile"),
        P(),
        P(None, "aperture", None),
        P(None, None, None, "aperture", None),
        P(None, None, "aperture"),
    )
    out_specs = P(None, "aperture", "tile")
    return jax.shard_map(
        on_device, mesh=mesh, in_specs=in_specs, out_specs=out_specs, check_vma=False
    )
```

```python
import jax
import jax.numpy as jnp
from jax import lax
from jax.experimental import pallas as pl
from jax.experimental.pallas import tpu as pltpu
from jax.sharding import PartitionSpec as P

BLOCK = 256
STEP = 512
VMEM = 48 * 1024 * 1024
LEAD = 3
LEVELS = 32767.0
WINDOW = 4
GROUP = 1024
NB = 16
BAND = 4
MESH = pl.DeviceIdType.MESH
EXACT = lax.Precision.HIGHEST
NT = (((1,), (1,)), ((), ()))


def kernel(n_tile, x_ref, taps_hbm, steer_hbm, coef_hbm, offs_hbm, out_ref,
           gathered, toep, rows, acc, mats, views, coded,
           taps_ref, steer_ref, coef_ref, offs_ref,
           x_send, x_recv, h_send, h_recv, p_send, p_recv, l_sem):
    width = x_ref.shape[2]
    span = taps_ref.shape[1]
    chunks = width // STEP
    step_rows = STEP // BLOCK * 64
    groups = width // GROUP
    per = GROUP // BLOCK
    group_rows = per * 64
    lags = span // GROUP
    ratio = GROUP // STEP
    d = lax.axis_index("aperture")
    t = lax.axis_index("tile")
    x = lax.rem(d, 4)
    base = d - x
    mate = (d, base + x + 1 - 2 * lax.rem(x, 2), base + lax.rem(x + 2, 4), base + 3 - x)
    before = lax.rem(t + n_tile - 1, n_tile)
    after = lax.rem(t + 1, n_tile)

    local = [
        pltpu.make_async_copy(src, dst, l_sem.at[k])
        for k, (src, dst) in enumerate(
            [(steer_hbm, steer_ref), (coef_hbm, coef_ref), (offs_hbm, offs_ref),
             (taps_hbm, taps_ref), (x_ref, gathered.at[0])]
        )
    ]
    barrier = pltpu.get_barrier_semaphore()
    for r in (1, 2, 3):
        pl.semaphore_signal(barrier, inc=1, device_id=(mate[r], t), device_id_type=MESH)
    for other in (before, after):
        pl.semaphore_signal(barrier, inc=1, device_id=(d, other), device_id_type=MESH)

    for copy in local:
        copy.start()
    pl.semaphore_wait(barrier, 5)

    def remote(src, dst, send, recv, where):
        return pltpu.make_async_remote_copy(
            src_ref=src, dst_ref=dst, send_sem=send, recv_sem=recv,
            device_id=where, device_id_type=MESH,
        )

    small = [
        remote(views.at[0], views.at[r], p_send.at[r], p_recv.at[r], (mate[r], t))
        for r in (1, 2, 3)
    ]
    small.append(remote(mats.at[0], mats.at[1], p_send.at[0], p_recv.at[0], (mate[2], t)))

    def own(c, r):
        at = pl.ds(c * STEP, STEP)
        return remote(
            x_ref.at[:, :, at], gathered.at[r, :, :, at], x_send.at[r, c], x_recv.at[r, c],
            (mate[r], t),
        )

    def onward(c):
        at = pl.ds(c * STEP, STEP)
        came, goes = (1, 3) if c % 2 == 0 else (3, 1)
        return remote(
            gathered.at[came, :, :, at], gathered.at[2, :, :, at], x_send.at[2, c],
            x_recv.at[2, c], (mate[goes], t),
        )

    def halo(q):
        return remote(
            coded.at[0, q], coded.at[1, q], h_send.at[q], h_recv.at[q], (d, before),
        )

    for c in range(WINDOW):
        for r in (1, 3):
            own(c, r).start()
    for copy in local[:4]:
        copy.wait()

    lane = lax.broadcasted_iota(jnp.int32, (NB, 128), 1)
    beam = lax.broadcasted_iota(jnp.int32, (NB, 128), 0)
    first = lax.rem(lane, 32) < 16
    group = lax.broadcasted_iota(jnp.int32, (32, 128), 1) // 32
    repeat = jnp.where(lax.rem(lane, 16) == beam, 1.0, 0.0)

    def flipped(s, k):
        offs = offs_ref[s].astype(jnp.float32)
        start = jnp.dot(offs, repeat, precision=EXACT, preferred_element_type=jnp.float32)
        real, imag = (
            jnp.dot(coef_ref[s, k, part], repeat, precision=EXACT, preferred_element_type=jnp.float32)
            for part in range(2)
        )
        top = jnp.zeros((NB, 128), jnp.float32)
        low = jnp.zeros((NB, 128), jnp.float32)
        for b in range(BAND):
            hit = beam.astype(jnp.float32) == start[k : k + 1] + float(b)
            re, im = real[b : b + 1], imag[b : b + 1]
            top += jnp.where(hit, jnp.where(first, re, im), 0.0)
            low += jnp.where(hit, jnp.where(first, -im, re), 0.0)
        return jnp.concatenate([top, low], axis=0)


    mats[0] = jnp.where(lax.rem(group, 2) == 0, flipped(0, 0), flipped(0, 1))
    place0 = jnp.where(lane == beam, 1.0, 0.0).astype(jnp.bfloat16)
    place1 = jnp.where(lane == beam + 16, 1.0, 0.0).astype(jnp.bfloat16)
    s_re, s_im = steer_ref[0], steer_ref[1]

    def put(value, where):
        return jnp.dot(value, where, preferred_element_type=jnp.float32)

    views[0] = jnp.concatenate(
        [put(s_re, place0) + put(s_im, place1), put(s_re, place1) - put(s_im, place0)], axis=0
    )
    for copy in small:
        copy.start()

    def build(part, lo, hi):
        line = taps_ref[part : part + 1, :].astype(jnp.float32)
        padded = jnp.concatenate(
            [jnp.zeros((1, 128), jnp.float32), line, jnp.zeros((1, 256), jnp.float32)], axis=1
        )
        wide = jnp.broadcast_to(padded, (16, span + 384))
        for s in range(lo, hi):
            turned = pltpu.roll(wide, s * 16, 1, stride=1, stride_axis=0).astype(jnp.bfloat16)
            toep[part, pl.ds(s * 16, 16), :] = turned[:, 128:]
            toep[part, pl.ds(128 + s * 16, 16), :] = turned[:, : span + 256]

    def stage(q):
        for g in range(groups):
            lag = q - g
            if lag < 0 or lag > lags:
                continue
            lo, hi = (0, 0) if lag == 0 else ((lag - 1) * per + 1, lag * per)
            left = jnp.concatenate(
                [rows[pl.ds((g * per + k) * 64, group_rows), :] for k in range(lo, hi + 1)], axis=1
            )
            for part in range(2):
                term = lax.dot_general(
                    left, toep[part, :, pl.ds(lo * BLOCK, (hi + 1 - lo) * BLOCK)], NT,
                    preferred_element_type=jnp.float32,
                )
                if lag == 0:
                    acc[part, pl.ds(g * group_rows, group_rows), :] = term
                else:
                    acc[part, pl.ds(g * group_rows, group_rows), :] += term

    def finish(g):
        for i in range(per):
            at = (g * per + i) * 64
            by_re = acc[0, pl.ds(at, 32), :] + acc[0, pl.ds(at + 32, 32), :]
            by_im = acc[1, pl.ds(at, 32), :] + acc[1, pl.ds(at + 32, 32), :]
            to = pl.ds((g * per + i) * BLOCK, BLOCK)
            out_ref[0, :, to] = by_re[:NB] - by_im[NB:]
            out_ref[1, :, to] = by_re[NB:] + by_im[:NB]

    def pass_on(c):
        for r in (1, 3):
            own(c, r).wait_recv()
        onward(c).start()
        if c + WINDOW < chunks:
            for r in (1, 3):
                own(c + WINDOW, r).start()

    def keep(at, value):
        high = value.astype(jnp.bfloat16)
        rows[pl.ds(at, 32), :] = high
        rows[pl.ds(at + 32, 32), :] = (value - high.astype(jnp.float32)).astype(jnp.bfloat16)

    def combine(c):
        onward(c).wait_recv()
        at = pl.ds(c * STEP, STEP)
        data = gathered[:, :, :, at].reshape(128, STEP)
        both = jnp.dot(w_both, data, preferred_element_type=jnp.float32)
        value = both[:32] + both[32:]
        for i in range(STEP // BLOCK):
            part = value[:, i * BLOCK : (i + 1) * BLOCK]
            keep(c * step_rows + i * 64, part)
            peak = jnp.maximum(jnp.max(jnp.abs(part), axis=1, keepdims=True), 1e-30)
            power = jnp.ceil(16.0 * jnp.log2(peak / LEVELS))
            level = jnp.round(part / jnp.exp2(power / 16.0))
            level = jnp.clip(level, -LEVELS, LEVELS)
            coded[0, c, :, pl.ds(i * BLOCK, BLOCK)] = level.astype(jnp.int32).astype(jnp.int16)
            coded[0, c, :, pl.ds(STEP + i * 128, 128)] = jnp.broadcast_to(
                power.astype(jnp.int32), (32, 128)
            ).astype(jnp.int16)

    def decode(q):
        for i in range(STEP // BLOCK):
            level = coded[1, q, :, pl.ds(i * BLOCK, BLOCK)].astype(jnp.int32).astype(jnp.float32)
            power = coded[1, q, :, pl.ds(STEP + i * 128, 128)].astype(jnp.int32)
            scale = jnp.exp2(power.astype(jnp.float32)[:, :1] / 16.0)
            keep((q + chunks) * step_rows + i * 64, level * scale)

    def make_weights():
        last = [jnp.concatenate([flipped(1, k)] * 4, axis=0) for k in range(2)]
        for copy in small:
            copy.wait_recv()
        columns = []
        for k in range(2):
            view = views[pl.ds(2 * k, 2)].reshape(64, 128)
            once = jnp.dot(
                view[:, :32], mats[k], precision=EXACT, preferred_element_type=jnp.float32
            )
            once = jnp.concatenate(
                [jnp.where(group == 0, once[:32], 0.0), jnp.where(group == 1, once[32:], 0.0)], axis=0
            )
            columns.append(
                jnp.dot(once, last[k], precision=EXACT, preferred_element_type=jnp.float32)
            )
        weights = jnp.concatenate(columns, axis=0).T[:32]
        w_high = weights.astype(jnp.bfloat16)
        w_low = (weights - w_high.astype(jnp.float32)).astype(jnp.bfloat16)
        w_both = jnp.concatenate([w_high, w_low], axis=0)
        return w_both

    todo = [(part, lo) for part in range(2) for lo in range(8)]

    def some(count):
        for _ in range(min(count, len(todo))):
            part, lo = todo.pop(0)
            build(part, lo, lo + 1)

    some(2)
    for c in range(LEAD):
        pass_on(c)
        some(3)
    w_both = make_weights()
    local[4].wait()
    done = 0
    for c in range(chunks):
        if c + LEAD < chunks:
            pass_on(c + LEAD)
        combine(c)

        @pl.when(t > 0)
        def _():
            halo(c).start()

        some(3)
        if not todo and (done + 1) * ratio <= c + 1:
            stage(done)
            done += 1
    for q in range(done, groups):
        stage(q)

    for q in range(groups):
        @pl.when(t < n_tile - 1)
        def _():
            for c in range(q * ratio, (q + 1) * ratio):
                halo(c).wait_recv()
                decode(c)

        @pl.when(t == n_tile - 1)
        def _():
            rows[pl.ds((q + groups) * group_rows, group_rows), :] = jnp.zeros(
                (group_rows, BLOCK), jnp.bfloat16
            )

        stage(q + groups)
        finish(q)

    for copy in small:
        copy.wait_send()
    for c in range(chunks):
        for r in (1, 3):
            own(c, r).wait_send()
        onward(c).wait_send()

        @pl.when(t > 0)
        def _():
            halo(c).wait_send()


def on_device(echoes, taps, steering, coefficients, offsets):
    width, span = echoes.shape[2], taps.shape[1]
    chunks = width // STEP
    blocks = (width + span) // BLOCK
    n_tile = lax.axis_size("tile")
    vmem = pl.BlockSpec(memory_space=pltpu.VMEM)
    dma = pltpu.SemaphoreType.DMA

    def body(*refs):
        kernel(n_tile, *refs)

    return pl.pallas_call(
        body,
        out_shape=jax.ShapeDtypeStruct((2, NB, width), jnp.float32),
        in_specs=[pl.BlockSpec(memory_space=pltpu.HBM)] * 5,
        out_specs=vmem,
        scratch_shapes=[
            pltpu.VMEM((4, 2, NB, width), jnp.bfloat16),
            pltpu.VMEM((2, BLOCK, span + BLOCK), jnp.bfloat16),
            pltpu.VMEM((blocks * 64, BLOCK), jnp.bfloat16),
            pltpu.VMEM((2, width // BLOCK * 64, BLOCK), jnp.float32),
            pltpu.VMEM((2, 32, 128), jnp.float32),
            pltpu.VMEM((4, 32, 128), jnp.float32),
            pltpu.VMEM((2, chunks, 32, STEP + STEP // BLOCK * 128), jnp.int16),
            pltpu.VMEM(taps.shape, taps.dtype),
            pltpu.VMEM(steering.shape, steering.dtype),
            pltpu.VMEM((2, 2, 2, BAND, NB), jnp.float32),
            pltpu.VMEM(offsets.shape, offsets.dtype),
            dma((4, chunks)),
            dma((4, chunks)),
            dma((chunks,)),
            dma((chunks,)),
            dma((4,)),
            dma((4,)),
            dma((5,)),
        ],
        compiler_params=pltpu.CompilerParams(
            collective_id=0, has_side_effects=True, vmem_limit_bytes=VMEM
        ),
        cost_estimate=pl.CostEstimate(
            flops=2 * 1024 * 256 * 256 * 34 * 2, bytes_accessed=1 << 20, transcendentals=0
        ),
        name="backproject",
    )(
        *(
            pltpu.with_memory_space_constraint(value, pltpu.HBM)
            for value in (echoes, taps, steering, jnp.swapaxes(coefficients, 3, 4), offsets)
        )
    )


def solution(mesh):
    in_specs = (
        P(None, "aperture", "tile"),
        P(),
        P(None, "aperture", None),
        P(None, None, None, "aperture", None),
        P(None, None, "aperture"),
    )
    out_specs = P(None, "aperture", "tile")
    return jax.shard_map(
        on_device, mesh=mesh, in_specs=in_specs, out_specs=out_specs, check_vma=False
    )
```

```python
import jax
import jax.numpy as jnp
from jax import lax
from jax.experimental import pallas as pl
from jax.experimental.pallas import tpu as pltpu
from jax.sharding import PartitionSpec as P

BLOCK = 256
STEP = 512
GROUP = 1024
AHEAD = 8
HLAG = 4
EARLY = 8
EACH = 2
LAG = 4
LEVELS = 32700.0
NB = 16
BAND = 4
MESH = pl.DeviceIdType.MESH
EXACT = lax.Precision.HIGHEST
NT = (((1,), (1,)), ((), ()))


def kernel(n_tile, x_hbm, taps_hbm, steer_hbm, coef_hbm, offs_hbm, out_ref,
           data, toep, rows, acc, parts, coded, coef, offs, steer, taps,
           x_send, x_recv, f_send, f_recv, h_send, h_recv, s_send, s_recv, l_sem):
    width = data.shape[3]
    span = taps.shape[1]
    chunks = width // STEP
    blocks = STEP // BLOCK
    step_rows = blocks * 64
    groups = width // GROUP
    per = GROUP // BLOCK
    group_rows = per * 64
    lags = span // GROUP
    ratio = GROUP // STEP
    d = lax.axis_index("aperture")
    t = lax.axis_index("tile")
    x = lax.rem(d, 4)
    next_to = (d + 1 - 2 * lax.rem(x, 2), t)
    across = (d - x + 3 - x, t)
    before = (d, lax.rem(t + n_tile - 1, n_tile))
    after = (d, lax.rem(t + 1, n_tile))

    barrier = pltpu.get_barrier_semaphore()
    for other in (next_to, across):
        pl.semaphore_signal(barrier, inc=1, device_id=other, device_id_type=MESH)

    @pl.when(t < n_tile - 1)
    def _():
        pl.semaphore_signal(barrier, inc=1, device_id=after, device_id_type=MESH)

    local = [
        pltpu.make_async_copy(src, dst, l_sem.at[k])
        for k, (src, dst) in enumerate(
            [(taps_hbm, taps), (steer_hbm, steer.at[0]), (coef_hbm, coef.at[0]),
             (offs_hbm, offs.at[0]), (x_hbm, data.at[0])]
        )
    ]
    for copy in local:
        copy.start()
    pl.semaphore_wait(barrier, jnp.where(t > 0, 3, 2))

    def remote(src, dst, send, recv, where):
        return pltpu.make_async_remote_copy(
            src_ref=src, dst_ref=dst, send_sem=send, recv_sem=recv,
            device_id=where, device_id_type=MESH,
        )

    small = [
        remote(src, dst, s_send.at[k], s_recv.at[k], where)
        for k, (src, dst, where) in enumerate(
            [(coef_hbm, coef.at[1], next_to), (offs_hbm, offs.at[1], next_to),
             (steer_hbm, steer.at[1], next_to), (coef_hbm, coef.at[2], across),
             (offs_hbm, offs.at[2], across)]
        )
    ]

    def own(c):
        at = pl.ds(c * STEP, STEP)
        return remote(
            x_hbm.at[:, :, at], data.at[1, :, :, at], x_send.at[c], x_recv.at[c], next_to
        )

    def share(c):
        return remote(coded.at[0, c], coded.at[1, c], f_send.at[c], f_recv.at[c], across)

    def halo(c):
        return remote(coded.at[2, c], coded.at[3, c], h_send.at[c], h_recv.at[c], before)

    for copy in small:
        copy.start()
    for c in range(AHEAD):
        own(c).start()

    def build(part, s):
        line = taps[part : part + 1, :].astype(jnp.float32)
        padded = jnp.concatenate(
            [jnp.zeros((1, 128), jnp.float32), line, jnp.zeros((1, 256), jnp.float32)], axis=1
        )
        wide = jnp.broadcast_to(padded, (16, span + 384))
        turned = pltpu.roll(wide, s * 16, 1, stride=1, stride_axis=0).astype(jnp.bfloat16)
        toep[part, pl.ds(s * 16, 16), :] = turned[:, 128:]
        toep[part, pl.ds(128 + s * 16, 16), :] = turned[:, : span + 256]

    lane = lax.broadcasted_iota(jnp.int32, (NB, 128), 1)
    beam = lax.broadcasted_iota(jnp.int32, (NB, 128), 0)
    first = lax.rem(lane, 32) < 16
    group = lax.broadcasted_iota(jnp.int32, (32, 128), 1) // 32
    repeat = jnp.where(lax.rem(lane, 16) == beam, 1.0, 0.0)
    place0 = jnp.where(lane == beam, 1.0, 0.0).astype(jnp.bfloat16)
    place1 = jnp.where(lane == beam + 16, 1.0, 0.0).astype(jnp.bfloat16)

    def times(left, right):
        return jnp.dot(left, right, precision=EXACT, preferred_element_type=jnp.float32)

    def flipped(who, s, k):
        start = times(offs[who, s].astype(jnp.float32), repeat)
        real, imag = (times(coef[who, s, k, part], repeat) for part in range(2))
        top = jnp.zeros((NB, 128), jnp.float32)
        low = jnp.zeros((NB, 128), jnp.float32)
        for b in range(BAND):
            hit = beam.astype(jnp.float32) == start[k : k + 1] + float(b)
            re, im = real[b : b + 1], imag[b : b + 1]
            top += jnp.where(hit, jnp.where(first, re, im), 0.0)
            low += jnp.where(hit, jnp.where(first, -im, re), 0.0)
        return jnp.concatenate([top, low], axis=0)

    def view(who):
        s_re, s_im = steer[who, 0], steer[who, 1]

        def put(value, where):
            return jnp.dot(value, where, preferred_element_type=jnp.float32)

        return jnp.concatenate(
            [put(s_re, place0) + put(s_im, place1), put(s_re, place1) - put(s_im, place0)], axis=0
        )

    def columns(pair, last, views):
        once = times(views[:, :32], jnp.where(lax.rem(group, 2) == 0, *pair))
        once = jnp.concatenate(
            [jnp.where(group == 0, once[:32], 0.0), jnp.where(group == 1, once[32:], 0.0)], axis=0
        )
        return times(once, jnp.concatenate([last] * 4, axis=0))

    def weights(view0, pair, last0):
        views = jnp.concatenate([view0, view(1)], axis=0)
        mine = columns(pair, last0, views)
        theirs = columns((flipped(1, 0, 1), flipped(1, 0, 0)), flipped(2, 1, 1), views)
        side = jnp.where(jnp.concatenate([group, group], axis=0) == 0, mine, theirs)
        whole = jnp.concatenate([side, jnp.zeros_like(side)], axis=0).T[:64, :64]
        high = whole.astype(jnp.bfloat16)
        low = (whole - high.astype(jnp.float32)).astype(jnp.bfloat16)
        return jnp.concatenate([high, low], axis=0)

    eye = lax.broadcasted_iota(jnp.int32, (32, 32), 0) == lax.broadcasted_iota(
        jnp.int32, (32, 32), 1
    )
    line = lax.broadcasted_iota(jnp.int32, (16, 32), 0)
    last = 2 * STEP // 128

    def encode(slot, c, values):
        powers = jnp.zeros((16, 32), jnp.float32)
        for i, value in enumerate(values):
            peak = jnp.maximum(jnp.max(jnp.abs(value), axis=1, keepdims=True), 1e-30)
            power = jnp.ceil(16.0 * jnp.log2(peak / LEVELS))
            level = jnp.round(value * jnp.exp2(power / -16.0)).astype(jnp.int32).astype(jnp.int16)
            for k in range(2):
                for m in range(BLOCK // 128):
                    coded[slot, c, 2 * (i * BLOCK // 128 + m) + k] = level[
                        k * 16 : (k + 1) * 16, m * 128 : (m + 1) * 128
                    ]
            across_lanes = jnp.sum(jnp.where(eye, power, 0.0), axis=0, keepdims=True)
            powers = jnp.where(line == i, across_lanes, powers)
        coded[slot, c, last, :, 0:32] = powers.astype(jnp.int32).astype(jnp.int16)

    def decode(slot, c):
        powers = coded[slot, c, last, :, 0:32].astype(jnp.int32).astype(jnp.float32)
        values = []
        for i in range(blocks):
            power = jnp.sum(jnp.where(eye, powers[i : i + 1], 0.0), axis=1, keepdims=True)
            level = jnp.concatenate(
                [
                    jnp.concatenate(
                        [coded[slot, c, 2 * (i * BLOCK // 128 + m) + k] for k in range(2)], axis=0
                    )
                    for m in range(BLOCK // 128)
                ],
                axis=1,
            )
            values.append(level.astype(jnp.int32).astype(jnp.float32) * jnp.exp2(power / 16.0))
        return values

    def keep(c, values):
        for i, value in enumerate(values):
            at = c * step_rows + i * 64
            high = value.astype(jnp.bfloat16)
            rows[pl.ds(at, 32), :] = high
            rows[pl.ds(at + 32, 32), :] = (value - high.astype(jnp.float32)).astype(jnp.bfloat16)

    def cut(value):
        return [value[:, i * BLOCK : (i + 1) * BLOCK] for i in range(blocks)]

    def combine(c, matrix):
        own(c).wait_recv()
        if c + AHEAD < chunks:
            own(c + AHEAD).start()
        at = pl.ds(c * STEP, STEP)
        both = jnp.dot(
            matrix, data[:, :, :, at].reshape(64, STEP), preferred_element_type=jnp.float32
        )
        value = both[:64] + both[64:]
        encode(0, c, cut(value[32:]))
        share(c).start()
        parts[:, at] = value[:32]

    def total(c):
        share(c).wait_recv()
        mine = cut(parts[:, pl.ds(c * STEP, STEP)])
        values = [a + b for a, b in zip(mine, decode(1, c))]
        encode(2, c, values)

        @pl.when(t > 0)
        def _():
            halo(c).start()

        keep(c, values)

    def stage(q, g):
        lag = q - g
        lo, hi = (0, 0) if lag == 0 else ((lag - 1) * per + 1, lag * per)
        left = jnp.concatenate(
            [rows[pl.ds((g * per + k) * 64, group_rows), :] for k in range(lo, hi + 1)], axis=1
        )
        for part in range(2):
            term = lax.dot_general(
                left, toep[part, :, pl.ds(lo * BLOCK, (hi + 1 - lo) * BLOCK)], NT,
                preferred_element_type=jnp.float32,
            )
            if lag == 0:
                acc[part, pl.ds(g * group_rows, group_rows), :] = term
            else:
                acc[part, pl.ds(g * group_rows, group_rows), :] += term

    def finish(g):
        for i in range(per):
            at = (g * per + i) * 64
            by_re = acc[0, pl.ds(at, 32), :] + acc[0, pl.ds(at + 32, 32), :]
            by_im = acc[1, pl.ds(at, 32), :] + acc[1, pl.ds(at + 32, 32), :]
            to = pl.ds((g * per + i) * BLOCK, BLOCK)
            out_ref[0, :, to] = by_re[:NB] - by_im[NB:]
            out_ref[1, :, to] = by_re[NB:] + by_im[:NB]

    todo = [(0, build, (part, s)) for s in range(8) for part in range(2)]
    todo += [((q + 1) * ratio, stage, (q, g)) for q in range(groups) for g in range(q + 1)]
    for q in range(groups):
        todo += [((q + 1 + groups) * ratio, stage, (q + groups, g)) for g in range(q, groups)]
        todo.append(((q + 1 + groups) * ratio, finish, (q,)))

    def some(count, summed, taken):
        for _ in range(count):
            need = todo[0][0] if todo else 3 * chunks
            if need <= summed or summed == chunks and need <= chunks + taken:
                _, call, given = todo.pop(0)
                call(*given)

    def take(c):
        @pl.when(t < n_tile - 1)
        def _():
            halo(c).wait_recv()
            keep(c + chunks, decode(3, c))

        @pl.when(t == n_tile - 1)
        def _():
            rows[pl.ds((c + chunks) * step_rows, step_rows), :] = jnp.zeros(
                (step_rows, BLOCK), jnp.bfloat16
            )

    for copy in local[1:4]:
        copy.wait()
    view0, pair, last0 = view(0), (flipped(0, 0, 0), flipped(0, 0, 1)), flipped(0, 1, 0)
    local[0].wait()
    some(EARLY, 0, 0)
    local[4].wait()
    for copy in small:
        copy.wait_recv()
    matrix = weights(view0, pair, last0)
    for c in range(chunks + LAG + HLAG):
        if c < chunks:
            combine(c, matrix)
        if 0 <= c - LAG < chunks:
            total(c - LAG)
        if c >= LAG + HLAG:
            take(c - LAG - HLAG)
        some(EACH, min(c + 1 - LAG, chunks), c + 1 - LAG - HLAG)
    some(len(todo), chunks, chunks)

    for copy in small:
        copy.wait_send()
    for c in range(chunks):
        own(c).wait_send()
        share(c).wait_send()

        @pl.when(t > 0)
        def _():
            halo(c).wait_send()


def on_device(echoes, taps, steering, coefficients, offsets):
    width, span = echoes.shape[2], taps.shape[1]
    chunks = width // STEP
    blocks = (width + span) // BLOCK
    n_tile = lax.axis_size("tile")
    small = jnp.swapaxes(coefficients, 3, 4)
    dma = pltpu.SemaphoreType.DMA

    def body(*refs):
        kernel(n_tile, *refs)

    return pl.pallas_call(
        body,
        out_shape=jax.ShapeDtypeStruct((2, NB, width), jnp.float32),
        in_specs=[pl.BlockSpec(memory_space=pltpu.HBM)] * 5,
        out_specs=pl.BlockSpec(memory_space=pltpu.VMEM),
        scratch_shapes=[
            pltpu.VMEM((2, 2, NB, width), jnp.bfloat16),
            pltpu.VMEM((2, BLOCK, span + BLOCK), jnp.bfloat16),
            pltpu.VMEM((blocks * 64, BLOCK), jnp.bfloat16),
            pltpu.VMEM((2, width // BLOCK * 64, BLOCK), jnp.float32),
            pltpu.VMEM((32, width), jnp.float32),
            pltpu.VMEM((4, chunks, 2 * STEP // 128 + 1, 16, 128), jnp.int16),
            pltpu.VMEM((3,) + small.shape, jnp.float32),
            pltpu.VMEM((3,) + offsets.shape, jnp.int32),
            pltpu.VMEM((2,) + steering.shape, jnp.bfloat16),
            pltpu.VMEM(taps.shape, jnp.bfloat16),
        ]
        + [dma((chunks,))] * 6
        + [dma((5,))] * 3,
        compiler_params=pltpu.CompilerParams(
            collective_id=0, has_side_effects=True, vmem_limit_bytes=48 * 1024 * 1024
        ),
        name="backproject",
    )(
        *(
            pltpu.with_memory_space_constraint(value, pltpu.HBM)
            for value in (echoes, taps, steering, small, offsets)
        )
    )


def solution(mesh):
    in_specs = (
        P(None, "aperture", "tile"),
        P(),
        P(None, "aperture", None),
        P(None, None, None, "aperture", None),
        P(None, None, "aperture"),
    )
    out_specs = P(None, "aperture", "tile")
    return jax.shard_map(
        on_device, mesh=mesh, in_specs=in_specs, out_specs=out_specs, check_vma=False
    )
```

```python
import jax
import jax.numpy as jnp
from jax import lax
from jax.experimental import pallas as pl
from jax.experimental.pallas import tpu as pltpu
from jax.sharding import PartitionSpec as P

BLOCK = 256
STEP = 512
GROUP = 1024
AHEAD = 8
HLAG = 4
EARLY = 8
EACH = 2
LAG = 4
LEVELS = 32700.0
NB = 16
BAND = 4
MESH = pl.DeviceIdType.MESH
EXACT = lax.Precision.HIGHEST
NT = (((1,), (1,)), ((), ()))


def kernel(n_tile, x_hbm, taps_hbm, steer_hbm, coef_hbm, offs_hbm, out_ref,
           data, toep, rows, acc, parts, coded, coef, offs, steer, taps,
           x_send, x_recv, f_send, f_recv, h_send, h_recv, s_send, s_recv, l_sem):
    width = data.shape[3]
    span = taps.shape[1]
    chunks = width // STEP
    blocks = STEP // BLOCK
    step_rows = blocks * 64
    groups = width // GROUP
    per = GROUP // BLOCK
    group_rows = per * 64
    lags = span // GROUP
    ratio = GROUP // STEP
    d = lax.axis_index("aperture")
    t = lax.axis_index("tile")
    x = lax.rem(d, 4)
    next_to = (d + 1 - 2 * lax.rem(x, 2), t)
    across = (d - x + 3 - x, t)
    before = (d, lax.rem(t + n_tile - 1, n_tile))
    after = (d, lax.rem(t + 1, n_tile))

    barrier = pltpu.get_barrier_semaphore()
    for other in (next_to, across):
        pl.semaphore_signal(barrier, inc=1, device_id=other, device_id_type=MESH)

    @pl.when(t < n_tile - 1)
    def _():
        pl.semaphore_signal(barrier, inc=1, device_id=after, device_id_type=MESH)

    local = [
        pltpu.make_async_copy(src, dst, l_sem.at[k])
        for k, (src, dst) in enumerate(
            [(taps_hbm, taps), (steer_hbm, steer.at[0]), (coef_hbm, coef.at[0]),
             (offs_hbm, offs.at[0]), (x_hbm, data.at[0])]
        )
    ]
    for copy in local:
        copy.start()
    pl.semaphore_wait(barrier, jnp.where(t > 0, 3, 2))

    def remote(src, dst, send, recv, where):
        return pltpu.make_async_remote_copy(
            src_ref=src, dst_ref=dst, send_sem=send, recv_sem=recv,
            device_id=where, device_id_type=MESH,
        )

    small = [
        remote(src, dst, s_send.at[k], s_recv.at[k], where)
        for k, (src, dst, where) in enumerate(
            [(coef_hbm, coef.at[1], next_to), (offs_hbm, offs.at[1], next_to),
             (steer_hbm, steer.at[1], next_to), (coef_hbm, coef.at[2], across),
             (offs_hbm, offs.at[2], across)]
        )
    ]

    def own(c):
        at = pl.ds(c * STEP, STEP)
        return remote(
            x_hbm.at[:, :, at], data.at[1, :, :, at], x_send.at[c], x_recv.at[c], next_to
        )

    def share(c):
        return remote(coded.at[0, c], coded.at[1, c], f_send.at[c], f_recv.at[c], across)

    def halo(c):
        return remote(coded.at[2, c], coded.at[3, c], h_send.at[c], h_recv.at[c], before)

    for copy in small:
        copy.start()
    for c in range(AHEAD):
        own(c).start()

    def build(part, s):
        line = taps[part : part + 1, :].astype(jnp.float32)
        padded = jnp.concatenate(
            [jnp.zeros((1, 128), jnp.float32), line, jnp.zeros((1, 256), jnp.float32)], axis=1
        )
        wide = jnp.broadcast_to(padded, (16, span + 384))
        turned = pltpu.roll(wide, s * 16, 1, stride=1, stride_axis=0).astype(jnp.bfloat16)
        toep[part, pl.ds(s * 16, 16), :] = turned[:, 128:]
        toep[part, pl.ds(128 + s * 16, 16), :] = turned[:, : span + 256]

    lane = lax.broadcasted_iota(jnp.int32, (NB, 128), 1)
    beam = lax.broadcasted_iota(jnp.int32, (NB, 128), 0)
    first = lax.rem(lane, 32) < 16
    group = lax.broadcasted_iota(jnp.int32, (32, 128), 1) // 32
    repeat = jnp.where(lax.rem(lane, 16) == beam, 1.0, 0.0)
    place0 = jnp.where(lane == beam, 1.0, 0.0).astype(jnp.bfloat16)
    place1 = jnp.where(lane == beam + 16, 1.0, 0.0).astype(jnp.bfloat16)

    def times(left, right):
        return jnp.dot(left, right, precision=EXACT, preferred_element_type=jnp.float32)

    def flipped(who, s, k):
        start = jnp.dot(
            offs[who, s].astype(jnp.float32).astype(jnp.bfloat16), repeat.astype(jnp.bfloat16),
            preferred_element_type=jnp.float32,
        )
        real, imag = (times(coef[who, s, k, part], repeat) for part in range(2))
        top = jnp.zeros((NB, 128), jnp.float32)
        low = jnp.zeros((NB, 128), jnp.float32)
        for b in range(BAND):
            hit = beam.astype(jnp.float32) == start[k : k + 1] + float(b)
            re, im = real[b : b + 1], imag[b : b + 1]
            top += jnp.where(hit, jnp.where(first, re, im), 0.0)
            low += jnp.where(hit, jnp.where(first, -im, re), 0.0)
        return jnp.concatenate([top, low], axis=0)

    def view(who):
        s_re, s_im = steer[who, 0], steer[who, 1]

        def put(value, where):
            return jnp.dot(value, where, preferred_element_type=jnp.float32)

        return jnp.concatenate(
            [put(s_re, place0) + put(s_im, place1), put(s_re, place1) - put(s_im, place0)], axis=0
        )

    def columns(pair, last, views):
        once = times(views[:, :32], jnp.where(lax.rem(group, 2) == 0, *pair))
        once = jnp.concatenate(
            [jnp.where(group == 0, once[:32], 0.0), jnp.where(group == 1, once[32:], 0.0)], axis=0
        )
        return times(once, jnp.concatenate([last] * 4, axis=0))

    def weights(view0, pair, last0):
        views = jnp.concatenate([view0, view(1)], axis=0)
        mine = columns(pair, last0, views)
        theirs = columns((flipped(1, 0, 1), flipped(1, 0, 0)), flipped(2, 1, 1), views)
        side = jnp.where(jnp.concatenate([group, group], axis=0) == 0, mine, theirs)
        whole = jnp.concatenate([side, jnp.zeros_like(side)], axis=0).T[:64, :64]
        high = whole.astype(jnp.bfloat16)
        low = (whole - high.astype(jnp.float32)).astype(jnp.bfloat16)
        return jnp.concatenate([high, low], axis=0)

    eye = lax.broadcasted_iota(jnp.int32, (32, 32), 0) == lax.broadcasted_iota(
        jnp.int32, (32, 32), 1
    )
    line = lax.broadcasted_iota(jnp.int32, (16, 32), 0)
    last = 2 * STEP // 128

    def encode(slot, c, values):
        powers = jnp.zeros((16, 32), jnp.float32)
        for i, value in enumerate(values):
            peak = jnp.maximum(jnp.max(jnp.abs(value), axis=1, keepdims=True), 1e-30)
            power = jnp.ceil(16.0 * jnp.log2(peak / LEVELS))
            level = jnp.round(value * jnp.exp2(power / -16.0)).astype(jnp.int32).astype(jnp.int16)
            for k in range(2):
                for m in range(BLOCK // 128):
                    coded[slot, c, 2 * (i * BLOCK // 128 + m) + k] = level[
                        k * 16 : (k + 1) * 16, m * 128 : (m + 1) * 128
                    ]
            across_lanes = jnp.sum(jnp.where(eye, power, 0.0), axis=0, keepdims=True)
            powers = jnp.where(line == i, across_lanes, powers)
        coded[slot, c, last, :, 0:32] = powers.astype(jnp.int32).astype(jnp.int16)

    def decode(slot, c):
        powers = coded[slot, c, last, :, 0:32].astype(jnp.int32).astype(jnp.float32)
        values = []
        for i in range(blocks):
            power = jnp.sum(jnp.where(eye, powers[i : i + 1], 0.0), axis=1, keepdims=True)
            level = jnp.concatenate(
                [
                    jnp.concatenate(
                        [coded[slot, c, 2 * (i * BLOCK // 128 + m) + k] for k in range(2)], axis=0
                    )
                    for m in range(BLOCK // 128)
                ],
                axis=1,
            )
            values.append(level.astype(jnp.int32).astype(jnp.float32) * jnp.exp2(power / 16.0))
        return values

    def keep(c, values):
        for i, value in enumerate(values):
            at = c * step_rows + i * 64
            high = value.astype(jnp.bfloat16)
            rows[pl.ds(at, 32), :] = high
            rows[pl.ds(at + 32, 32), :] = (value - high.astype(jnp.float32)).astype(jnp.bfloat16)

    def cut(value):
        return [value[:, i * BLOCK : (i + 1) * BLOCK] for i in range(blocks)]

    def combine(c, matrix):
        own(c).wait_recv()
        if c + AHEAD < chunks:
            own(c + AHEAD).start()
        at = pl.ds(c * STEP, STEP)
        both = jnp.dot(
            matrix, data[:, :, :, at].reshape(64, STEP), preferred_element_type=jnp.float32
        )
        value = both[:64] + both[64:]
        encode(0, c, cut(value[32:]))
        share(c).start()
        parts[:, at] = value[:32]

    def total(c):
        share(c).wait_recv()
        mine = cut(parts[:, pl.ds(c * STEP, STEP)])
        values = [a + b for a, b in zip(mine, decode(1, c))]
        encode(2, c, values)

        @pl.when(t > 0)
        def _():
            halo(c).start()

        keep(c, values)

    def stage(q, g):
        lag = q - g
        lo, hi = (0, 0) if lag == 0 else ((lag - 1) * per + 1, lag * per)
        left = jnp.concatenate(
            [rows[pl.ds((g * per + k) * 64, group_rows), :] for k in range(lo, hi + 1)], axis=1
        )
        for part in range(2):
            term = lax.dot_general(
                left, toep[part, :, pl.ds(lo * BLOCK, (hi + 1 - lo) * BLOCK)], NT,
                preferred_element_type=jnp.float32,
            )
            if lag == 0:
                acc[part, pl.ds(g * group_rows, group_rows), :] = term
            else:
                acc[part, pl.ds(g * group_rows, group_rows), :] += term

    def finish(g):
        for i in range(per):
            at = (g * per + i) * 64
            by_re = acc[0, pl.ds(at, 32), :] + acc[0, pl.ds(at + 32, 32), :]
            by_im = acc[1, pl.ds(at, 32), :] + acc[1, pl.ds(at + 32, 32), :]
            to = pl.ds((g * per + i) * BLOCK, BLOCK)
            out_ref[0, :, to] = by_re[:NB] - by_im[NB:]
            out_ref[1, :, to] = by_re[NB:] + by_im[:NB]

    todo = [(0, build, (part, s)) for s in range(8) for part in range(2)]
    todo += [((q + 1) * ratio, stage, (q, g)) for q in range(groups) for g in range(q + 1)]
    for q in range(groups):
        todo += [((q + 1 + groups) * ratio, stage, (q + groups, g)) for g in range(q, groups)]
        todo.append(((q + 1 + groups) * ratio, finish, (q,)))

    def some(count, summed, taken):
        for _ in range(count):
            need = todo[0][0] if todo else 3 * chunks
            if need <= summed or summed == chunks and need <= chunks + taken:
                _, call, given = todo.pop(0)
                call(*given)

    def take(c):
        @pl.when(t < n_tile - 1)
        def _():
            halo(c).wait_recv()
            keep(c + chunks, decode(3, c))

        @pl.when(t == n_tile - 1)
        def _():
            rows[pl.ds((c + chunks) * step_rows, step_rows), :] = jnp.zeros(
                (step_rows, BLOCK), jnp.bfloat16
            )

    for copy in local[1:4]:
        copy.wait()
    view0, pair, last0 = view(0), (flipped(0, 0, 0), flipped(0, 0, 1)), flipped(0, 1, 0)
    local[0].wait()
    some(EARLY, 0, 0)
    local[4].wait()
    for copy in small:
        copy.wait_recv()
    matrix = weights(view0, pair, last0)
    for c in range(chunks + LAG + HLAG):
        if c < chunks:
            combine(c, matrix)
        if 0 <= c - LAG < chunks:
            total(c - LAG)
        if c >= LAG + HLAG:
            take(c - LAG - HLAG)
        some(EACH, min(c + 1 - LAG, chunks), c + 1 - LAG - HLAG)
    some(len(todo), chunks, chunks)

    for copy in small:
        copy.wait_send()
    for c in range(chunks):
        own(c).wait_send()
        share(c).wait_send()

        @pl.when(t > 0)
        def _():
            halo(c).wait_send()


def on_device(echoes, taps, steering, coefficients, offsets):
    width, span = echoes.shape[2], taps.shape[1]
    chunks = width // STEP
    blocks = (width + span) // BLOCK
    n_tile = lax.axis_size("tile")
    small = jnp.swapaxes(coefficients, 3, 4)
    dma = pltpu.SemaphoreType.DMA

    def body(*refs):
        kernel(n_tile, *refs)

    return pl.pallas_call(
        body,
        out_shape=jax.ShapeDtypeStruct((2, NB, width), jnp.float32),
        in_specs=[pl.BlockSpec(memory_space=pltpu.HBM)] * 5,
        out_specs=pl.BlockSpec(memory_space=pltpu.VMEM),
        scratch_shapes=[
            pltpu.VMEM((2, 2, NB, width), jnp.bfloat16),
            pltpu.VMEM((2, BLOCK, span + BLOCK), jnp.bfloat16),
            pltpu.VMEM((blocks * 64, BLOCK), jnp.bfloat16),
            pltpu.VMEM((2, width // BLOCK * 64, BLOCK), jnp.float32),
            pltpu.VMEM((32, width), jnp.float32),
            pltpu.VMEM((4, chunks, 2 * STEP // 128 + 1, 16, 128), jnp.int16),
            pltpu.VMEM((3,) + small.shape, jnp.float32),
            pltpu.VMEM((3,) + offsets.shape, jnp.int32),
            pltpu.VMEM((2,) + steering.shape, jnp.bfloat16),
            pltpu.VMEM(taps.shape, jnp.bfloat16),
        ]
        + [dma((chunks,))] * 6
        + [dma((5,))] * 3,
        compiler_params=pltpu.CompilerParams(
            collective_id=0, has_side_effects=True, vmem_limit_bytes=48 * 1024 * 1024
        ),
        name="backproject",
    )(
        *(
            pltpu.with_memory_space_constraint(value, pltpu.HBM)
            for value in (echoes, taps, steering, small, offsets)
        )
    )


def solution(mesh):
    in_specs = (
        P(None, "aperture", "tile"),
        P(),
        P(None, "aperture", None),
        P(None, None, None, "aperture", None),
        P(None, None, "aperture"),
    )
    out_specs = P(None, "aperture", "tile")
    return jax.shard_map(
        on_device, mesh=mesh, in_specs=in_specs, out_specs=out_specs, check_vma=False
    )
```
